256 devices in a mesh: gy: 16 (over z, y_lo), gz: 16 (over x, y_hi, core).
Axes of the slice: x: 4, y: 4 (y_hi: 2, y_lo: 2; y = y_hi * 2 + y_lo), z: 8, core: 2. Of those that a mesh axis runs over, the one named last changes fastest.
Arguments:
- wave_field: float32 [2, 2, 256, 256, 256], P(None, None, 'gy', 'gz'), may hold values from -2.5 to 2.5
- trap_field: float32 [256, 256, 256], P('gy', 'gz'), may hold values from 0 to 1.5
Outputs:
- wave_next: float32 [2, 2, 256, 256, 256], P(None, None, 'gy', 'gz')
- momentum_image: float32 [256, 256, 256], P('gy', 'gz')
The draws below stay inside these ranges and needn't reach their ends.
All inputs are finite; a program needn't handle non-finite values.
Results may differ from the reference program's by a relative error of at most 0.0003.
Values sent between devices are 32-bit elements; how exact they have to be, the bound alone decides.
A program may use at most 128 MiB of HBM per device.

```python
import jax
import jax.numpy as jnp
from jax import lax

NX = 256
NY = 256
NZ = 256


def level_of(own_key, dims, split, smallest, largest):
    gain, own = 1.0, jax.random.fold_in(own_key, 6)
    for axis_at, parts in split:
        heights = jnp.exp(jax.random.uniform(jax.random.fold_in(own, axis_at), (parts,), jnp.float32, smallest / len(split), largest / len(split)))
        gain = gain * jnp.repeat(heights, dims[axis_at] // parts).reshape([-1 if axis == axis_at else 1 for axis in range(len(dims))])
    return gain


def gaussian(stream_key, extent, spread, bound, pieces=(), kind=jnp.bfloat16):
    gain = level_of(stream_key, extent, pieces, -0.22, 0.18) if pieces else 1.0
    result = jax.random.normal(stream_key, extent, jnp.float32) * spread * gain
    return jnp.minimum(jnp.maximum(result, -bound), bound).astype(kind)


def setup_inputs(seed: int = 0) -> dict:
    key_list = jax.random.split(jax.random.key(seed), 3)
    return {
        "wave_field": gaussian(key_list[0], (2, 2, NY, NZ, NX), 1.0, 2.5, ((2, 16), (3, 16)), jnp.float32),
        "trap_field": jnp.clip(1.5 * jax.random.uniform(key_list[1], (NY, NZ, NX), jnp.float32) ** level_of(key_list[1], (NY, NZ, NX), ((0, 16), (1, 16)), -0.2, 0.2), 0.0, 1.5),
    }


hopping = 1.5
time_step = 0.1
rabi_rate = 0.8
inter_self_first = 0.1
inter_cross = 0.06
inter_self_second = 0.08
block_rows = 16


def trimmed(values, margin):
    return values[..., margin:values.shape[-3] - margin, margin:values.shape[-2] - margin, :]


def derivative(padded, trap_part):
    center = trimmed(padded, 1)
    beside = padded[:, :, 2:, 1:-1] + padded[:, :, :-2, 1:-1]
    beside = beside + padded[:, :, 1:-1, 2:] + padded[:, :, 1:-1, :-2]
    beside = beside + jnp.roll(center, 1, axis=4) + jnp.roll(center, -1, axis=4)
    density = center[:, 0] * center[:, 0] + center[:, 1] * center[:, 1]
    level_first = trap_part + inter_self_first * density[0] + inter_cross * density[1]
    level_second = trap_part + inter_cross * density[0] + inter_self_second * density[1]
    levels = jnp.stack([level_first, level_second])[:, None]
    applied = levels * center - hopping * beside - (0.5 * rabi_rate) * center[::-1]
    return jnp.stack([applied[:, 1], -applied[:, 0]], axis=1)


def runge_kutta(extended, trap_wide):
    slope_one = derivative(extended, trap_wide)
    state_one = trimmed(extended, 1) + (0.5 * time_step) * slope_one
    slope_two = derivative(state_one, trimmed(trap_wide, 1))
    state_two = trimmed(extended, 2) + (0.5 * time_step) * slope_two
    slope_three = derivative(state_two, trimmed(trap_wide, 2))
    state_three = trimmed(extended, 3) + time_step * slope_three
    slope_four = derivative(state_three, trimmed(trap_wide, 3))
    return trimmed(extended, 4) + (time_step / 6.0) * (trimmed(slope_one, 3) + 2.0 * trimmed(slope_two, 2) + 2.0 * trimmed(slope_three, 1) + slope_four)


def reference(wave_field, trap_field):
    padded = jnp.pad(wave_field, ((0, 0), (0, 0), (4, 4), (4, 4), (0, 0)), mode="wrap")
    trap_padded = jnp.pad(trap_field, ((3, 3), (3, 3), (0, 0)), mode="wrap")
    block_count = NY // block_rows

    def one_block(block_index):
        first_row = (block_index * block_rows).astype(jnp.int32)
        extended = lax.dynamic_slice_in_dim(padded, first_row, block_rows + 8, 2)
        trap_wide = lax.dynamic_slice_in_dim(trap_padded, first_row, block_rows + 6, 0)
        return runge_kutta(extended, trap_wide)

    blocks = lax.map(one_block, jnp.arange(block_count, dtype=jnp.int32))
    wave_next = jnp.moveaxis(blocks, 0, 2).reshape(2, 2, NY, NZ, NX)
    total_power = jnp.zeros((NY, NZ, NX), jnp.float32)
    for component in range(2):
        complex_field = lax.complex(wave_next[component, 0], wave_next[component, 1])
        spectrum = jnp.fft.fftn(complex_field)
        total_power = total_power + (jnp.real(spectrum) ** 2 + jnp.imag(spectrum) ** 2)
    momentum_image = jnp.transpose(total_power, (2, 0, 1)) / float(NX * NY * NZ)
    return wave_next, momentum_image
```

```python
import math

import jax
import jax.numpy as jnp
import numpy as np
from jax import lax
from jax.experimental import pallas as pl
from jax.experimental.pallas import tpu as pltpu
from jax.sharding import PartitionSpec as P

MESH = pl.DeviceIdType.MESH

hopping = 1.5
time_step = 0.1
rabi_rate = 0.8
inter_self_first = 0.1
inter_cross = 0.06
inter_self_second = 0.08

CHUNKS = 4


def rotation(angle):
    c, s = np.cos(angle), np.sin(angle)
    return np.stack([np.stack([c, s]), np.stack([-s, c])])


def in_two(table):
    table = table.astype(np.float32)
    high = table.astype(jnp.bfloat16)
    low = (table - high.astype(np.float32)).astype(jnp.bfloat16)
    return np.stack([high, low])


def tables(n):
    size, half = n * n, n // 2
    i = np.arange(size)
    full = rotation(2.0 * np.pi * ((i[:, None] * i[None, :]) % size) / size)
    one = full.reshape(2, 2, n, 2, half, size).transpose(3, 2, 0, 4, 1, 5)
    one = one.reshape(2, size, 2 * size)
    j = np.arange(n)
    small = rotation(2.0 * np.pi * ((j[:, None] * j[None, :]) % n) / n)
    two = np.einsum("opay,zw->aozpyw", small, np.eye(n)).reshape(2 * size, 2 * size)
    three = full.reshape(2, 2, size, n, n).transpose(0, 2, 3, 1, 4).reshape(2 * size, 2 * size)
    turn = 2.0 * np.pi * (j[:, None] * j[None, :]) / size
    turn = np.repeat(turn, n, axis=1)
    twiddle = np.stack([np.cos(turn), np.sin(turn)], axis=1).astype(np.float32)
    return in_two(one), in_two(two), in_two(three), twiddle


def fourier(values):
    count = len(values)
    if count == 1:
        return values
    even, odd = fourier(values[0::2]), fourier(values[1::2])
    first, second = [], []
    for k in range(count // 2):
        (er, ei), (r, i) = even[k], odd[k]
        if k == 0:
            tr, ti = r, i
        elif 4 * k == count:
            tr, ti = i, -r
        else:
            c, s = math.cos(2.0 * math.pi * k / count), math.sin(2.0 * math.pi * k / count)
            if 8 * k == count:
                tr, ti = c * (r + i), c * (i - r)
            elif 8 * k == 3 * count:
                tr, ti = s * (i - r), -s * (r + i)
            else:
                tr, ti = c * r + s * i, c * i - s * r
        first.append((er + tr, ei + ti))
        second.append((er - tr, ei - ti))
    return first + second


def split(value):
    high = value.astype(jnp.bfloat16)
    return high, (value - high.astype(jnp.float32)).astype(jnp.bfloat16)


def product(table, high, low, dims):
    def dot(a, b):
        return lax.dot_general(a, b, (dims, ((), ())), preferred_element_type=jnp.float32)

    return dot(table[0], high) + (dot(table[0], low) + dot(table[1], high))


NT = ((1,), (1,))
NN = ((1,), (0,))


def kernel(
    n, wave_hbm, trap_hbm, one_hbm, two_hbm, three_hbm, twiddle_hbm,
    next_hbm, image_ref,
    state, face_out, face_in, trap, wave_next, field, one, two, three, twiddle,
    sent_y, got_y, mixed, sent_z, got_z,
    load_sem, store_sem, halo_send, halo_recv, y_send, y_recv, z_send, z_recv,
):
    size, half = n * n, n // 2
    gy, gz = lax.axis_index("gy"), lax.axis_index("gz")

    def in_y(d):
        return (lax.rem(gy + d, n), gz)

    def in_z(d):
        return (gy, lax.rem(gz + d, n))

    barrier = pltpu.get_barrier_semaphore()

    def greet(d, carry):
        pl.semaphore_signal(barrier, inc=1, device_id=in_y(d), device_id_type=MESH)
        pl.semaphore_signal(barrier, inc=1, device_id=in_z(d), device_id_type=MESH)
        return carry

    lax.fori_loop(1, n, greet, 0)

    loads = [
        pltpu.make_async_copy(wave_hbm, state.at[0, :, pl.ds(1, n)], load_sem.at[0]),
        pltpu.make_async_copy(trap_hbm, trap, load_sem.at[1]),
        pltpu.make_async_copy(one_hbm, one, load_sem.at[2]),
        pltpu.make_async_copy(two_hbm, two, load_sem.at[3]),
        pltpu.make_async_copy(three_hbm, three, load_sem.at[4]),
        pltpu.make_async_copy(twiddle_hbm, twiddle, load_sem.at[5]),
    ]
    for load in loads:
        load.start()
    loads[0].wait()

    def y_faces(s):
        up = pltpu.make_async_remote_copy(
            src_ref=state.at[s, :, pl.ds(n, 1)], dst_ref=state.at[s, :, pl.ds(0, 1)],
            send_sem=halo_send.at[s, 0], recv_sem=halo_recv.at[s, 0],
            device_id=in_y(1), device_id_type=MESH,
        )
        down = pltpu.make_async_remote_copy(
            src_ref=state.at[s, :, pl.ds(1, 1)], dst_ref=state.at[s, :, pl.ds(n + 1, 1)],
            send_sem=halo_send.at[s, 1], recv_sem=halo_recv.at[s, 1],
            device_id=in_y(n - 1), device_id_type=MESH,
        )
        return up, down

    def z_faces(s):
        up = pltpu.make_async_remote_copy(
            src_ref=face_out.at[s, 1], dst_ref=face_in.at[s, 0],
            send_sem=halo_send.at[s, 2], recv_sem=halo_recv.at[s, 2],
            device_id=in_z(1), device_id_type=MESH,
        )
        down = pltpu.make_async_remote_copy(
            src_ref=face_out.at[s, 0], dst_ref=face_in.at[s, 1],
            send_sem=halo_send.at[s, 3], recv_sem=halo_recv.at[s, 3],
            device_id=in_z(n - 1), device_id_type=MESH,
        )
        return up, down

    pl.semaphore_wait(barrier, 2 * (n - 1))
    for copy in y_faces(0):
        copy.start()

    def first_faces(y, carry):
        for i in range(4):
            plane = state[0, i, y + 1]
            face_out[0, 0, i, pl.ds(y, 1), :] = plane[0:1]
            face_out[0, 1, i, pl.ds(y, 1), :] = plane[n - 1 : n]
        return carry

    lax.fori_loop(0, n, first_faces, 0)
    for copy in z_faces(0):
        copy.start()
    loads[1].wait()

    row = lax.broadcasted_iota(jnp.int32, (n, size), 0)

    def slope(s, y):
        center = [state[s, i, y + 1] for i in range(4)]
        density = [
            center[0] * center[0] + center[1] * center[1],
            center[2] * center[2] + center[3] * center[3],
        ]
        base = trap[y]
        level = [
            base + inter_self_first * density[0] + inter_cross * density[1],
            base + inter_cross * density[0] + inter_self_second * density[1],
        ]
        applied = []
        for i in range(4):
            mid = center[i]
            beside = state[s, i, y + 2] + state[s, i, y]
            before = face_in[s, 0, i, pl.ds(y, 1), :]
            after = face_in[s, 1, i, pl.ds(y, 1), :]
            beside += jnp.where(row == 0, before, pltpu.roll(mid, 1, 0))
            beside += jnp.where(row == n - 1, after, pltpu.roll(mid, n - 1, 0))
            beside += pltpu.roll(mid, 1, 1) + pltpu.roll(mid, size - 1, 1)
            applied.append(
                level[i // 2] * mid - hopping * beside - 0.5 * rabi_rate * center[(i + 2) % 4]
            )
        return [applied[1], -applied[0], applied[3], -applied[2]]

    for s in range(4):
        for copy in y_faces(s) + z_faces(s):
            copy.wait_recv()

        if s < 3:
            step = (0.5 * time_step, 0.5 * time_step, time_step)[s]

            def plane(y, s=s, step=step):
                for i, change in enumerate(slope(s, y)):
                    new = state[0, i, y + 1] + step * change
                    state[s + 1, i, y + 1] = new
                    face_out[s + 1, 0, i, pl.ds(y, 1), :] = new[0:1]
                    face_out[s + 1, 1, i, pl.ds(y, 1), :] = new[n - 1 : n]

            def outer(j, carry):
                plane(j * (n - 1))
                return carry

            def inner(y, carry):
                plane(y)
                return carry

            lax.fori_loop(0, 2, outer, 0)
            for copy in y_faces(s + 1):
                copy.start()
            lax.fori_loop(1, n - 1, inner, 0)
            for copy in z_faces(s + 1):
                copy.start()
        else:

            def last(y, carry):
                for i, change in enumerate(slope(3, y)):
                    kept = (
                        state[1, i, y + 1] + state[3, i, y + 1] - state[0, i, y + 1]
                        + 2.0 * state[2, i, y + 1]
                    )
                    new = kept * (1.0 / 3.0) + (time_step / 6.0) * change
                    wave_next[i, y] = new
                    high, low = split(new)
                    rows = pl.ds(pl.multiple_of(y * n, n), n)
                    field[0, i // 2, rows, (i % 2) * size : (i % 2 + 1) * size] = high
                    field[1, i // 2, rows, (i % 2) * size : (i % 2 + 1) * size] = low
                return carry

            lax.fori_loop(0, n, last, 0)

    store = pltpu.make_async_copy(wave_next, next_hbm, store_sem)
    store.start()

    def y_copy(ch, d):
        return pltpu.make_async_remote_copy(
            src_ref=sent_y.at[ch, lax.rem(gy + d, n)], dst_ref=got_y.at[ch, gy],
            send_sem=y_send.at[ch, d], recv_sem=y_recv.at[ch, d],
            device_id=in_y(d), device_id_type=MESH,
        )

    def z_copy(ch, d):
        return pltpu.make_async_remote_copy(
            src_ref=sent_z.at[ch, lax.rem(gz + d, n)], dst_ref=got_z.at[ch, gz],
            send_sem=z_send.at[ch, d], recv_sem=z_recv.at[ch, d],
            device_id=in_z(d), device_id_type=MESH,
        )

    def start_all(copy, ch):
        def one_start(j, carry):
            away = j // 2 + 1
            copy(ch, lax.rem(n + away * (1 - 2 * (j % 2)), n)).start()
            return carry

        lax.fori_loop(0, n - 1, one_start, 0)

    def arrived(copy, ch):
        def one_wait(d, carry):
            copy(ch, d).wait_recv()
            return carry

        lax.fori_loop(1, n, one_wait, 0)

    loads[2].wait()

    def along_x(ch, carry):
        c, h = ch % 2, ch // 2
        out = product((one[0, h], one[1, h]), field[0, c], field[1, c], NT)
        sent_y[ch] = out.reshape(n, n, size)
        start_all(y_copy, ch)
        got_y[ch, gy] = sent_y[ch, gy]
        return carry

    lax.fori_loop(0, CHUNKS, along_x, 0)

    loads[3].wait()
    loads[5].wait()

    def along_y(ch, carry):
        arrived(y_copy, ch)
        lanes = size // 2
        for part in range(2):
            at = slice(part * lanes, (part + 1) * lanes)
            values = [(got_y[ch, s, 0:half, at], got_y[ch, s, half:n, at]) for s in range(n)]
            values = fourier(values)
            for b in range(0, n, 2):
                turned = []
                for k in (b, b + 1):
                    (re, im), cos, sin = values[k], twiddle[k, 0:1, at], twiddle[k, 1:2, at]
                    turned.append((re * cos + im * sin, im * cos - re * sin))
                for p in range(2):
                    both = jnp.concatenate([turned[0][p], turned[1][p]], axis=0)
                    high, low = split(both)
                    to = slice(p * size + part * lanes, p * size + (part + 1) * lanes)
                    mixed[0, b * half : (b + 2) * half, to] = high
                    mixed[1, b * half : (b + 2) * half, to] = low
        out = product((two[0], two[1]), mixed[0], mixed[1], NT)
        sent_z[ch] = out.reshape(n, 2 * n, size // 2)
        start_all(z_copy, ch)
        got_z[ch, gz] = sent_z[ch, gz]
        return carry

    lax.fori_loop(0, CHUNKS, along_y, 0)

    loads[4].wait()

    def along_z(h, carry):
        power = None
        for c in range(2):
            ch = 2 * h + c
            arrived(z_copy, ch)
            high, low = split(got_z[ch].reshape(2 * size, size // 2))
            out = product((three[0], three[1]), high, low, NN)
            re, im = out[:size], out[size:]
            new = re * re + im * im
            power = new if power is None else power + new
        image_ref[h] = (power * (1.0 / float(size**3))).T
        return carry

    lax.fori_loop(0, 2, along_z, 0)

    for s in range(4):
        for copy in y_faces(s) + z_faces(s):
            copy.wait_send()

    def sent(j, carry):
        for ch in range(CHUNKS):
            y_copy(ch, j).wait_send()
            z_copy(ch, j).wait_send()
        return carry

    lax.fori_loop(1, n, sent, 0)
    store.wait()


def solution(mesh):
    n = mesh.shape["gy"]
    size, half = n * n, n // 2
    arrays = tables(n)

    def body(wave_field, trap_field):
        f32, bf16 = jnp.float32, jnp.bfloat16
        dma = pltpu.SemaphoreType.DMA
        wave_next, image = pl.pallas_call(
            lambda *refs: kernel(n, *refs),
            out_shape=(
                jax.ShapeDtypeStruct((4, n, n, size), f32),
                jax.ShapeDtypeStruct((2, size // 2, size), f32),
            ),
            in_specs=[pl.BlockSpec(memory_space=pl.ANY)] * 6,
            out_specs=(
                pl.BlockSpec(memory_space=pl.ANY),
                pl.BlockSpec(memory_space=pltpu.VMEM),
            ),
            scratch_shapes=[
                pltpu.VMEM((4, 4, n + 2, n, size), f32),
                pltpu.VMEM((4, 2, 4, n, size), f32),
                pltpu.VMEM((4, 2, 4, n, size), f32),
                pltpu.VMEM((n, n, size), f32),
                pltpu.VMEM((4, n, n, size), f32),
                pltpu.VMEM((2, 2, size, 2 * size), bf16),
                pltpu.VMEM((2, 2, size, 2 * size), bf16),
                pltpu.VMEM((2, 2 * size, 2 * size), bf16),
                pltpu.VMEM((2, 2 * size, 2 * size), bf16),
                pltpu.VMEM((n, 2, size), f32),
                pltpu.VMEM((CHUNKS, n, n, size), f32),
                pltpu.VMEM((CHUNKS, n, n, size), f32),
                pltpu.VMEM((2, size // 2, 2 * size), bf16),
                pltpu.VMEM((CHUNKS, n, 2 * n, size // 2), f32),
                pltpu.VMEM((CHUNKS, n, 2 * n, size // 2), f32),
                dma((6,)),
                dma(()),
                dma((4, 4)),
                dma((4, 4)),
                dma((CHUNKS, n)),
                dma((CHUNKS, n)),
                dma((CHUNKS, n)),
                dma((CHUNKS, n)),
            ],
            compiler_params=pltpu.CompilerParams(
                collective_id=0, has_side_effects=True, vmem_limit_bytes=48 * 1024 * 1024
            ),
        )(wave_field.reshape(4, n, n, size), trap_field, *(jnp.asarray(a) for a in arrays))
        image = image.reshape(2, n, half, size).transpose(0, 2, 1, 3).reshape(n, n, size)
        return wave_next.reshape(2, 2, n, n, size), image

    return jax.shard_map(
        body,
        mesh=mesh,
        in_specs=(P(None, None, "gy", "gz", None), P("gy", "gz", None)),
        out_specs=(P(None, None, "gy", "gz", None), P("gy", "gz", None)),
        check_vma=False,
    )
```

```python
import math

import jax
import jax.numpy as jnp
import numpy as np
from jax import lax
from jax.experimental import pallas as pl
from jax.experimental.pallas import tpu as pltpu
from jax.sharding import PartitionSpec as P

MESH = pl.DeviceIdType.MESH

hopping = 1.5
time_step = 0.1
rabi_rate = 0.8
inter_self_first = 0.1
inter_cross = 0.06
inter_self_second = 0.08

CHUNKS = 4


def rotation(angle):
    c, s = np.cos(angle), np.sin(angle)
    return np.stack([np.stack([c, s]), np.stack([-s, c])])


def in_two(table):
    table = table.astype(np.float32)
    high = table.astype(jnp.bfloat16)
    low = (table - high.astype(np.float32)).astype(jnp.bfloat16)
    return np.stack([high, low])


def tables(n):
    size, half = n * n, n // 2
    i = np.arange(size)
    full = rotation(2.0 * np.pi * ((i[:, None] * i[None, :]) % size) / size)
    one = full.reshape(2, 2, n, 2, half, size).transpose(3, 2, 0, 4, 1, 5)
    one = one.reshape(2, size, 2 * size)
    j = np.arange(n)
    small = rotation(2.0 * np.pi * ((j[:, None] * j[None, :]) % n) / n)
    two = np.einsum("opay,zw->aozpyw", small, np.eye(n)).reshape(2 * size, 2 * size)
    three = full.reshape(2, 2, size, n, n).transpose(0, 2, 3, 1, 4).reshape(2 * size, 2 * size)
    turn = 2.0 * np.pi * (j[:, None] * j[None, :]) / size
    turn = np.repeat(turn, n, axis=1)
    twiddle = np.stack([np.cos(turn), np.sin(turn)], axis=1).astype(np.float32)
    return in_two(one), in_two(two), in_two(three), twiddle


def fourier(values):
    count = len(values)
    if count == 1:
        return values
    even, odd = fourier(values[0::2]), fourier(values[1::2])
    first, second = [], []
    for k in range(count // 2):
        (er, ei), (r, i) = even[k], odd[k]
        if k == 0:
            tr, ti = r, i
        elif 4 * k == count:
            tr, ti = i, -r
        else:
            c, s = math.cos(2.0 * math.pi * k / count), math.sin(2.0 * math.pi * k / count)
            if 8 * k == count:
                tr, ti = c * (r + i), c * (i - r)
            elif 8 * k == 3 * count:
                tr, ti = s * (i - r), -s * (r + i)
            else:
                tr, ti = c * r + s * i, c * i - s * r
        first.append((er + tr, ei + ti))
        second.append((er - tr, ei - ti))
    return first + second


def split(value):
    high = value.astype(jnp.bfloat16)
    return high, (value - high.astype(jnp.float32)).astype(jnp.bfloat16)


def product(table, high, low, dims):
    def dot(a, b):
        return lax.dot_general(a, b, (dims, ((), ())), preferred_element_type=jnp.float32)

    return dot(table[0], high) + (dot(table[0], low) + dot(table[1], high))


NT = ((1,), (1,))
NN = ((1,), (0,))


def kernel(
    n, wave_hbm, trap_hbm, one_hbm, two_hbm, three_hbm, twiddle_hbm,
    next_hbm, image_ref,
    state0, state1, state2, state3, out0, out1, out2, out3, in0, in1, in2, in3, trap, wave_next, field, one, two, three, twiddle,
    sent_y, got_y, mixed, sent_z, got_z, power,
    load_sem, store_sem, halo_send, halo_recv, y_send, y_recv, z_send, z_recv,
):
    size, half = n * n, n // 2
    state = (state0, state1, state2, state3)
    face_out, face_in = (out0, out1, out2, out3), (in0, in1, in2, in3)
    gy, gz = lax.axis_index("gy"), lax.axis_index("gz")

    def in_y(d):
        return (lax.rem(gy + d, n), gz)

    def in_z(d):
        return (gy, lax.rem(gz + d, n))

    loads = [
        pltpu.make_async_copy(wave_hbm, state[0].at[:, pl.ds(1, n)], load_sem.at[0]),
        pltpu.make_async_copy(trap_hbm, trap, load_sem.at[1]),
        pltpu.make_async_copy(one_hbm, one, load_sem.at[2]),
        pltpu.make_async_copy(two_hbm, two, load_sem.at[3]),
        pltpu.make_async_copy(three_hbm, three, load_sem.at[4]),
        pltpu.make_async_copy(twiddle_hbm, twiddle, load_sem.at[5]),
    ]
    loads[0].start()
    barrier = pltpu.get_barrier_semaphore()

    def greet(d, carry):
        pl.semaphore_signal(barrier, inc=1, device_id=in_y(d), device_id_type=MESH)
        pl.semaphore_signal(barrier, inc=1, device_id=in_z(d), device_id_type=MESH)
        return carry

    lax.fori_loop(1, n, greet, 0)
    for load in loads[1:]:
        load.start()

    groups = ((0, 2), (2, n // 2), (n // 2, n))

    def y_faces(s):
        up = pltpu.make_async_remote_copy(
            src_ref=state[s].at[:, pl.ds(n, 1)], dst_ref=state[s].at[:, pl.ds(0, 1)],
            send_sem=halo_send.at[s, 0], recv_sem=halo_recv.at[s, 0],
            device_id=in_y(1), device_id_type=MESH,
        )
        down = pltpu.make_async_remote_copy(
            src_ref=state[s].at[:, pl.ds(1, 1)], dst_ref=state[s].at[:, pl.ds(n + 1, 1)],
            send_sem=halo_send.at[s, 1], recv_sem=halo_recv.at[s, 1],
            device_id=in_y(n - 1), device_id_type=MESH,
        )
        return up, down

    def z_faces(s, g):
        first, end = groups[g]
        part = pl.ds(first, end - first)
        up = pltpu.make_async_remote_copy(
            src_ref=face_out[s].at[1, part], dst_ref=face_in[s].at[0, part],
            send_sem=halo_send.at[s, 2 + 2 * g], recv_sem=halo_recv.at[s, 2 + 2 * g],
            device_id=in_z(1), device_id_type=MESH,
        )
        down = pltpu.make_async_remote_copy(
            src_ref=face_out[s].at[0, part], dst_ref=face_in[s].at[1, part],
            send_sem=halo_send.at[s, 3 + 2 * g], recv_sem=halo_recv.at[s, 3 + 2 * g],
            device_id=in_z(n - 1), device_id_type=MESH,
        )
        return up, down

    def over_planes(g, do, together=2):
        first, end = groups[g]

        def some(q, carry):
            js = [first + together * q + k for k in range(together)]
            do([(j, j * (n - 1) if g == 0 else j - 1) for j in js])
            return carry

        lax.fori_loop(0, (end - first) // together, some, 0)

    def keep_faces(s, j, i, plane):
        face_out[s][0, j, i : i + 1, :] = plane[0:1]
        face_out[s][1, j, i : i + 1, :] = plane[n - 1 : n]

    loads[0].wait()

    def first_faces(planes):
        for j, y in planes:
            for i in range(4):
                keep_faces(0, j, i, state[0][i, y + 1])

    for g in range(3):
        over_planes(g, first_faces)
    pl.semaphore_wait(barrier, 2 * (n - 1))
    for copy in y_faces(0) + z_faces(0, 0) + z_faces(0, 1) + z_faces(0, 2):
        copy.start()
    loads[1].wait()

    row = lax.broadcasted_iota(jnp.int32, (n, size), 0)

    def slope(s, j, y, components=(0, 1)):
        center = [state[s][i, y + 1] for i in range(4)]
        density = [
            center[0] * center[0] + center[1] * center[1],
            center[2] * center[2] + center[3] * center[3],
        ]
        base = trap[y]
        change = {}
        for c in components:
            own, cross = ((inter_self_first, inter_cross), (inter_cross, inter_self_second))[c]
            level = base + own * density[0] + cross * density[1]
            applied = []
            for i in (2 * c, 2 * c + 1):
                mid = center[i]
                before = face_in[s][0, j, i : i + 1, :]
                after = face_in[s][1, j, i : i + 1, :]
                beside = state[s][i, y + 2] + state[s][i, y]
                beside += jnp.where(row == 0, before, pltpu.roll(mid, 1, 0))
                beside += jnp.where(row == n - 1, after, pltpu.roll(mid, n - 1, 0))
                beside += pltpu.roll(mid, 1, 1) + pltpu.roll(mid, size - 1, 1)
                applied.append(
                    level * mid - hopping * beside - 0.5 * rabi_rate * center[(i + 2) % 4]
                )
            change[2 * c], change[2 * c + 1] = applied[1], -applied[0]
        return change

    for s in range(3):
        step = (0.5 * time_step, 0.5 * time_step, time_step)[s]

        def advance(planes, s=s, step=step):
            made = []
            for j, y in planes:
                for i, change in slope(s, j, y).items():
                    made.append((j, y, i, state[0][i, y + 1] + step * change))
            for j, y, i, new in made:
                state[s + 1][i, y + 1] = new
                keep_faces(s + 1, j, i, new)

        for g in range(3):
            for copy in z_faces(s, g) + (y_faces(s) if g == 0 else ()):
                copy.wait_recv()
            over_planes(g, advance)
            for copy in (y_faces(s + 1) if g == 0 else ()) + z_faces(s + 1, g):
                copy.start()

    def y_copy(ch, d):
        return pltpu.make_async_remote_copy(
            src_ref=sent_y.at[ch, lax.rem(gy + d, n)], dst_ref=got_y.at[ch, gy],
            send_sem=y_send.at[ch, d], recv_sem=y_recv.at[ch, d],
            device_id=in_y(d), device_id_type=MESH,
        )

    def z_copy(ch, d):
        return pltpu.make_async_remote_copy(
            src_ref=sent_z.at[ch, lax.rem(gz + d, n)], dst_ref=got_z.at[ch, gz],
            send_sem=z_send.at[ch, d], recv_sem=z_recv.at[ch, d],
            device_id=in_z(d), device_id_type=MESH,
        )

    def start_all(copy, ch):
        def one_start(j, carry):
            away = j // 2 + 1
            copy(ch, lax.rem(n + away * (1 - 2 * (j % 2)), n)).start()
            return carry

        lax.fori_loop(0, n - 1, one_start, 0)

    def arrived(copy, ch):
        def one_wait(d, carry):
            copy(ch, d).wait_recv()
            return carry

        lax.fori_loop(1, n, one_wait, 0)

    for c in range(2):

        def last(planes, c=c):
            made = []
            for j, y in planes:
                for i, change in slope(3, j, y, (c,)).items():
                    kept = (
                        state[1][i, y + 1] + state[3][i, y + 1] - state[0][i, y + 1]
                        + 2.0 * state[2][i, y + 1]
                    )
                    made.append((y, i, kept * (1.0 / 3.0) + (time_step / 6.0) * change))
            for y, i, new in made:
                wave_next[i, y] = new
                high, low = split(new)
                rows = pl.ds(pl.multiple_of(y * n, n), n)
                field[0, c, rows, (i % 2) * size : (i % 2 + 1) * size] = high
                field[1, c, rows, (i % 2) * size : (i % 2 + 1) * size] = low

        for g in range(3):
            if c == 0:
                for copy in z_faces(3, g) + (y_faces(3) if g == 0 else ()):
                    copy.wait_recv()
            over_planes(g, last)
        if c == 0:
            loads[2].wait()

        def along_x(h, carry, c=c):
            ch = 2 * c + h
            out = product((one[0, h], one[1, h]), field[0, c], field[1, c], NT)
            sent_y[ch] = out.reshape(n, n, size)
            start_all(y_copy, ch)
            got_y[ch, gy] = sent_y[ch, gy]
            return carry

        lax.fori_loop(0, 2, along_x, 0)

    store = pltpu.make_async_copy(wave_next, next_hbm, store_sem)
    store.start()

    loads[3].wait()
    loads[5].wait()

    def along_y(ch, carry):
        arrived(y_copy, ch)
        lanes = size // 2
        for part in range(2):
            at = slice(part * lanes, (part + 1) * lanes)
            values = [(got_y[ch, s, 0:half, at], got_y[ch, s, half:n, at]) for s in range(n)]
            values = fourier(values)
            for b in range(0, n, 2):
                turned = []
                for k in (b, b + 1):
                    (re, im), cos, sin = values[k], twiddle[k, 0:1, at], twiddle[k, 1:2, at]
                    turned.append((re * cos + im * sin, im * cos - re * sin))
                for p in range(2):
                    both = jnp.concatenate([turned[0][p], turned[1][p]], axis=0)
                    high, low = split(both)
                    to = slice(p * size + part * lanes, p * size + (part + 1) * lanes)
                    mixed[0, b * half : (b + 2) * half, to] = high
                    mixed[1, b * half : (b + 2) * half, to] = low
        out = product((two[0], two[1]), mixed[0], mixed[1], NT)
        sent_z[ch] = out.reshape(n, 2 * n, size // 2)
        start_all(z_copy, ch)
        got_z[ch, gz] = sent_z[ch, gz]
        return carry

    lax.fori_loop(0, CHUNKS, along_y, 0)

    loads[4].wait()

    for c in range(2):

        def along_z(h, carry, c=c):
            ch = 2 * c + h
            arrived(z_copy, ch)
            high, low = split(got_z[ch].reshape(2 * size, size // 2))
            out = product((three[0], three[1]), high, low, NN)
            re, im = out[:size], out[size:]
            new = re * re + im * im
            if c == 0:
                power[h] = new
            else:
                image_ref[h] = ((power[h] + new) * (1.0 / float(size**3))).T
            return carry

        lax.fori_loop(0, 2, along_z, 0)

    for s in range(4):
        for copy in y_faces(s) + z_faces(s, 0) + z_faces(s, 1) + z_faces(s, 2):
            copy.wait_send()

    def sent(j, carry):
        for ch in range(CHUNKS):
            y_copy(ch, j).wait_send()
            z_copy(ch, j).wait_send()
        return carry

    lax.fori_loop(1, n, sent, 0)
    store.wait()


def solution(mesh):
    n = mesh.shape["gy"]
    size, half = n * n, n // 2
    arrays = tables(n)

    def body(wave_field, trap_field):
        f32, bf16 = jnp.float32, jnp.bfloat16
        dma = pltpu.SemaphoreType.DMA
        wave_next, image = pl.pallas_call(
            lambda *refs: kernel(n, *refs),
            out_shape=(
                jax.ShapeDtypeStruct((4, n, n, size), f32),
                jax.ShapeDtypeStruct((2, size // 2, size), f32),
            ),
            in_specs=[pl.BlockSpec(memory_space=pltpu.HBM)] * 6,
            out_specs=(
                pl.BlockSpec(memory_space=pltpu.HBM),
                pl.BlockSpec(memory_space=pltpu.VMEM),
            ),
            scratch_shapes=[
                *[pltpu.VMEM((4, n + 2, n, size), f32)] * 4,
                *[pltpu.VMEM((2, n, 4, size), f32)] * 8,
                pltpu.VMEM((n, n, size), f32),
                pltpu.VMEM((4, n, n, size), f32),
                pltpu.VMEM((2, 2, size, 2 * size), bf16),
                pltpu.VMEM((2, 2, size, 2 * size), bf16),
                pltpu.VMEM((2, 2 * size, 2 * size), bf16),
                pltpu.VMEM((2, 2 * size, 2 * size), bf16),
                pltpu.VMEM((n, 2, size), f32),
                pltpu.VMEM((CHUNKS, n, n, size), f32),
                pltpu.VMEM((CHUNKS, n, n, size), f32),
                pltpu.VMEM((2, size // 2, 2 * size), bf16),
                pltpu.VMEM((CHUNKS, n, 2 * n, size // 2), f32),
                pltpu.VMEM((CHUNKS, n, 2 * n, size // 2), f32),
                pltpu.VMEM((2, size, size // 2), f32),
                dma((6,)),
                dma(()),
                dma((4, 8)),
                dma((4, 8)),
                dma((CHUNKS, n)),
                dma((CHUNKS, n)),
                dma((CHUNKS, n)),
                dma((CHUNKS, n)),
            ],
            compiler_params=pltpu.CompilerParams(
                collective_id=0, has_side_effects=True, vmem_limit_bytes=60 * 1024 * 1024
            ),
        )(wave_field.reshape(4, n, n, size), trap_field, *(jnp.asarray(a) for a in arrays))
        image = image.reshape(2, n, half, size).transpose(0, 2, 1, 3).reshape(n, n, size)
        return wave_next.reshape(2, 2, n, n, size), image

    return jax.shard_map(
        body,
        mesh=mesh,
        in_specs=(P(None, None, "gy", "gz", None), P("gy", "gz", None)),
        out_specs=(P(None, None, "gy", "gz", None), P("gy", "gz", None)),
        check_vma=False,
    )
```

```python
import math

import jax
import jax.numpy as jnp
import numpy as np
from jax import lax
from jax.experimental import pallas as pl
from jax.experimental.pallas import tpu as pltpu
from jax.sharding import PartitionSpec as P

MESH = pl.DeviceIdType.MESH

hopping = 1.5
time_step = 0.1
rabi_rate = 0.8
inter_self_first = 0.1
inter_cross = 0.06
inter_self_second = 0.08

CHUNKS = 4


def rotation(angle):
    c, s = np.cos(angle), np.sin(angle)
    return np.stack([np.stack([c, s]), np.stack([-s, c])])


def in_two(table):
    table = table.astype(np.float32)
    high = table.astype(jnp.bfloat16)
    low = (table - high.astype(np.float32)).astype(jnp.bfloat16)
    return np.stack([high, low])


def tables(n):
    size, half = n * n, n // 2
    i = np.arange(size)
    full = rotation(2.0 * np.pi * ((i[:, None] * i[None, :]) % size) / size)
    one = full.reshape(2, 2, n, 2, half, size).transpose(3, 2, 0, 4, 1, 5)
    one = one.reshape(2, size, 2 * size)
    j = np.arange(n)
    small = rotation(2.0 * np.pi * ((j[:, None] * j[None, :]) % n) / n)
    two = np.einsum("opay,zw->aozpyw", small, np.eye(n)).reshape(2 * size, 2 * size)
    three = full.reshape(2, 2, size, n, n).transpose(0, 2, 3, 1, 4).reshape(2 * size, 2 * size)
    turn = 2.0 * np.pi * (j[:, None] * j[None, :]) / size
    turn = np.repeat(turn, n, axis=1)
    twiddle = np.stack([np.cos(turn), np.sin(turn)], axis=1).astype(np.float32)
    return in_two(one), in_two(two), in_two(three), twiddle


def fourier(values):
    count = len(values)
    if count == 1:
        return values
    even, odd = fourier(values[0::2]), fourier(values[1::2])
    first, second = [], []
    for k in range(count // 2):
        (er, ei), (r, i) = even[k], odd[k]
        if k == 0:
            tr, ti = r, i
        elif 4 * k == count:
            tr, ti = i, -r
        else:
            c, s = math.cos(2.0 * math.pi * k / count), math.sin(2.0 * math.pi * k / count)
            if 8 * k == count:
                tr, ti = c * (r + i), c * (i - r)
            elif 8 * k == 3 * count:
                tr, ti = s * (i - r), -s * (r + i)
            else:
                tr, ti = c * r + s * i, c * i - s * r
        first.append((er + tr, ei + ti))
        second.append((er - tr, ei - ti))
    return first + second


def split(value):
    high = value.astype(jnp.bfloat16)
    return high, (value - high.astype(jnp.float32)).astype(jnp.bfloat16)


def product(table, high, low, dims):
    def dot(a, b):
        return lax.dot_general(a, b, (dims, ((), ())), preferred_element_type=jnp.float32)

    return dot(table[0], high) + (dot(table[0], low) + dot(table[1], high))


NT = ((1,), (1,))
NN = ((1,), (0,))


def kernel(
    n, wave_hbm, trap_hbm, one_hbm, two_hbm, three_hbm, twiddle_hbm,
    next_hbm, image_ref,
    state0, state1, state2, state3, out0, out1, out2, out3, in0, in1, in2, in3, trap, wave_next, field, one, two, three, twiddle,
    sent_y, got_y, mixed, sent_z, got_z, power,
    load_sem, store_sem, halo_send, halo_recv, y_send, y_recv, z_send, z_recv,
):
    size, half = n * n, n // 2
    state = (state0, state1, state2, state3)
    face_out, face_in = (out0, out1, out2, out3), (in0, in1, in2, in3)
    gy, gz = lax.axis_index("gy"), lax.axis_index("gz")

    def in_y(d):
        return (lax.rem(gy + d, n), gz)

    def in_z(d):
        return (gy, lax.rem(gz + d, n))

    loads = [
        pltpu.make_async_copy(wave_hbm, state[0].at[:, pl.ds(1, n)], load_sem.at[0]),
        pltpu.make_async_copy(trap_hbm, trap, load_sem.at[1]),
        pltpu.make_async_copy(one_hbm, one, load_sem.at[2]),
        pltpu.make_async_copy(two_hbm, two, load_sem.at[3]),
        pltpu.make_async_copy(three_hbm, three, load_sem.at[4]),
        pltpu.make_async_copy(twiddle_hbm, twiddle, load_sem.at[5]),
    ]
    loads[0].start()
    barrier = pltpu.get_barrier_semaphore()

    def greet(d, carry):
        pl.semaphore_signal(barrier, inc=1, device_id=in_y(d), device_id_type=MESH)
        pl.semaphore_signal(barrier, inc=1, device_id=in_z(d), device_id_type=MESH)
        return carry

    lax.fori_loop(1, n, greet, 0)
    for load in loads[1:]:
        load.start()

    groups = ((0, 2), (2, n // 2), (n // 2, n))

    def y_faces(s):
        up = pltpu.make_async_remote_copy(
            src_ref=state[s].at[:, pl.ds(n, 1)], dst_ref=state[s].at[:, pl.ds(0, 1)],
            send_sem=halo_send.at[s, 0], recv_sem=halo_recv.at[s, 0],
            device_id=in_y(1), device_id_type=MESH,
        )
        down = pltpu.make_async_remote_copy(
            src_ref=state[s].at[:, pl.ds(1, 1)], dst_ref=state[s].at[:, pl.ds(n + 1, 1)],
            send_sem=halo_send.at[s, 1], recv_sem=halo_recv.at[s, 1],
            device_id=in_y(n - 1), device_id_type=MESH,
        )
        return up, down

    def z_faces(s, g):
        first, end = groups[g]
        part = pl.ds(first, end - first)
        up = pltpu.make_async_remote_copy(
            src_ref=face_out[s].at[1, part], dst_ref=face_in[s].at[0, part],
            send_sem=halo_send.at[s, 2 + 2 * g], recv_sem=halo_recv.at[s, 2 + 2 * g],
            device_id=in_z(1), device_id_type=MESH,
        )
        down = pltpu.make_async_remote_copy(
            src_ref=face_out[s].at[0, part], dst_ref=face_in[s].at[1, part],
            send_sem=halo_send.at[s, 3 + 2 * g], recv_sem=halo_recv.at[s, 3 + 2 * g],
            device_id=in_z(n - 1), device_id_type=MESH,
        )
        return up, down

    def over_planes(g, do, together=2):
        first, end = groups[g]

        def some(q, carry):
            js = [first + together * q + k for k in range(together)]
            do([(j, j * (n - 1) if g == 0 else j - 1) for j in js])
            return carry

        lax.fori_loop(0, (end - first) // together, some, 0)

    def keep_faces(s, j, i, plane):
        face_out[s][0, j, i : i + 1, :] = plane[0:1]
        face_out[s][1, j, i : i + 1, :] = plane[n - 1 : n]

    loads[0].wait()

    def first_faces(planes):
        for j, y in planes:
            for i in range(4):
                keep_faces(0, j, i, state[0][i, y + 1])

    for g in range(3):
        over_planes(g, first_faces)
    pl.semaphore_wait(barrier, 2 * (n - 1))
    for copy in y_faces(0) + z_faces(0, 0) + z_faces(0, 1) + z_faces(0, 2):
        copy.start()
    loads[1].wait()

    row = lax.broadcasted_iota(jnp.int32, (n, size), 0)

    def slope(s, j, y, components=(0, 1)):
        center = [state[s][i, y + 1] for i in range(4)]
        density = [
            center[0] * center[0] + center[1] * center[1],
            center[2] * center[2] + center[3] * center[3],
        ]
        base = trap[y]
        change = {}
        for c in components:
            own, cross = ((inter_self_first, inter_cross), (inter_cross, inter_self_second))[c]
            level = base + own * density[0] + cross * density[1]
            applied = []
            for i in (2 * c, 2 * c + 1):
                mid = center[i]
                before = face_in[s][0, j, i : i + 1, :]
                after = face_in[s][1, j, i : i + 1, :]
                beside = state[s][i, y + 2] + state[s][i, y]
                beside += jnp.where(row == 0, before, pltpu.roll(mid, 1, 0))
                beside += jnp.where(row == n - 1, after, pltpu.roll(mid, n - 1, 0))
                beside += pltpu.roll(mid, 1, 1) + pltpu.roll(mid, size - 1, 1)
                applied.append(
                    level * mid - hopping * beside - 0.5 * rabi_rate * center[(i + 2) % 4]
                )
            change[2 * c], change[2 * c + 1] = applied[1], -applied[0]
        return change

    for s in range(3):
        step = (0.5 * time_step, 0.5 * time_step, time_step)[s]

        def advance(planes, s=s, step=step):
            made = []
            for j, y in planes:
                for i, change in slope(s, j, y).items():
                    made.append((j, y, i, state[0][i, y + 1] + step * change))
            for j, y, i, new in made:
                state[s + 1][i, y + 1] = new
                keep_faces(s + 1, j, i, new)

        for g in range(3):
            for copy in z_faces(s, g) + (y_faces(s) if g == 0 else ()):
                copy.wait_recv()
            over_planes(g, advance)
            for copy in (y_faces(s + 1) if g == 0 else ()) + z_faces(s + 1, g):
                copy.start()

    def y_copy(ch, d):
        return pltpu.make_async_remote_copy(
            src_ref=sent_y.at[ch, lax.rem(gy + d, n)], dst_ref=got_y.at[ch, gy],
            send_sem=y_send.at[ch, d], recv_sem=y_recv.at[ch, d],
            device_id=in_y(d), device_id_type=MESH,
        )

    def z_copy(ch, d):
        return pltpu.make_async_remote_copy(
            src_ref=sent_z.at[ch, lax.rem(gz + d, n)], dst_ref=got_z.at[ch, gz],
            send_sem=z_send.at[ch, d], recv_sem=z_recv.at[ch, d],
            device_id=in_z(d), device_id_type=MESH,
        )

    def start_all(copy, ch):
        def one_start(j, carry):
            away = j // 2 + 1
            copy(ch, lax.rem(n + away * (1 - 2 * (j % 2)), n)).start()
            return carry

        lax.fori_loop(0, n - 1, one_start, 0)

    def arrived(copy, ch):
        def one_wait(d, carry):
            copy(ch, d).wait_recv()
            return carry

        lax.fori_loop(1, n, one_wait, 0)

    for c in range(2):

        def last(planes, c=c):
            made = []
            for j, y in planes:
                for i, change in slope(3, j, y, (c,)).items():
                    kept = (
                        state[1][i, y + 1] + state[3][i, y + 1] - state[0][i, y + 1]
                        + 2.0 * state[2][i, y + 1]
                    )
                    made.append((y, i, kept * (1.0 / 3.0) + (time_step / 6.0) * change))
            for y, i, new in made:
                wave_next[i, y] = new
                high, low = split(new)
                rows = pl.ds(pl.multiple_of(y * n, n), n)
                field[0, c, rows, (i % 2) * size : (i % 2 + 1) * size] = high
                field[1, c, rows, (i % 2) * size : (i % 2 + 1) * size] = low

        for g in range(3):
            if c == 0:
                for copy in z_faces(3, g) + (y_faces(3) if g == 0 else ()):
                    copy.wait_recv()
            over_planes(g, last)
        if c == 0:
            loads[2].wait()

        def along_x(h, carry, c=c):
            ch = 2 * c + h
            out = product((one[0, h], one[1, h]), field[0, c], field[1, c], NT)
            sent_y[ch] = out.reshape(n, n, size)
            start_all(y_copy, ch)
            got_y[ch, gy] = sent_y[ch, gy]
            return carry

        lax.fori_loop(0, 2, along_x, 0)

    store = pltpu.make_async_copy(wave_next, next_hbm, store_sem)
    store.start()

    loads[3].wait()
    loads[5].wait()

    def along_y(ch, carry):
        arrived(y_copy, ch)
        lanes = size // 2
        for part in range(2):
            at = slice(part * lanes, (part + 1) * lanes)
            values = [(got_y[ch, s, 0:half, at], got_y[ch, s, half:n, at]) for s in range(n)]
            values = fourier(values)
            for b in range(0, n, 2):
                turned = []
                for k in (b, b + 1):
                    (re, im), cos, sin = values[k], twiddle[k, 0:1, at], twiddle[k, 1:2, at]
                    turned.append((re * cos + im * sin, im * cos - re * sin))
                for p in range(2):
                    both = jnp.concatenate([turned[0][p], turned[1][p]], axis=0)
                    high, low = split(both)
                    to = slice(p * size + part * lanes, p * size + (part + 1) * lanes)
                    mixed[0, b * half : (b + 2) * half, to] = high
                    mixed[1, b * half : (b + 2) * half, to] = low
        out = product((two[0], two[1]), mixed[0], mixed[1], NT)
        sent_z[ch] = out.reshape(n, 2 * n, size // 2)
        start_all(z_copy, ch)
        got_z[ch, gz] = sent_z[ch, gz]
        return carry

    lax.fori_loop(0, CHUNKS, along_y, 0)

    loads[4].wait()

    for c in range(2):

        def along_z(h, carry, c=c):
            ch = 2 * c + h
            arrived(z_copy, ch)
            high, low = split(got_z[ch].reshape(2 * size, size // 2))
            out = product((three[0], three[1]), high, low, NN)
            re, im = out[:size], out[size:]
            new = re * re + im * im
            if c == 0:
                power[h] = new
            else:
                image_ref[h] = ((power[h] + new) * (1.0 / float(size**3))).T
            return carry

        lax.fori_loop(0, 2, along_z, 0)

    for s in range(4):
        for copy in y_faces(s) + z_faces(s, 0) + z_faces(s, 1) + z_faces(s, 2):
            copy.wait_send()

    def sent(j, carry):
        for ch in range(CHUNKS):
            y_copy(ch, j).wait_send()
            z_copy(ch, j).wait_send()
        return carry

    lax.fori_loop(1, n, sent, 0)
    store.wait()


def solution(mesh):
    n = mesh.shape["gy"]
    size, half = n * n, n // 2
    arrays = tables(n)

    def body(wave_field, trap_field):
        f32, bf16 = jnp.float32, jnp.bfloat16
        dma = pltpu.SemaphoreType.DMA
        wave_next, image = pl.pallas_call(
            lambda *refs: kernel(n, *refs),
            out_shape=(
                jax.ShapeDtypeStruct((4, n, n, size), f32),
                jax.ShapeDtypeStruct((2, size // 2, size), f32),
            ),
            in_specs=[pl.BlockSpec(memory_space=pltpu.HBM)] * 6,
            out_specs=(
                pl.BlockSpec(memory_space=pltpu.HBM),
                pl.BlockSpec(memory_space=pltpu.VMEM),
            ),
            scratch_shapes=[
                *[pltpu.VMEM((4, n + 2, n, size), f32)] * 4,
                *[pltpu.VMEM((2, n, 4, size), f32)] * 8,
                pltpu.VMEM((n, n, size), f32),
                pltpu.VMEM((4, n, n, size), f32),
                pltpu.VMEM((2, 2, size, 2 * size), bf16),
                pltpu.VMEM((2, 2, size, 2 * size), bf16),
                pltpu.VMEM((2, 2 * size, 2 * size), bf16),
                pltpu.VMEM((2, 2 * size, 2 * size), bf16),
                pltpu.VMEM((n, 2, size), f32),
                pltpu.VMEM((CHUNKS, n, n, size), f32),
                pltpu.VMEM((CHUNKS, n, n, size), f32),
                pltpu.VMEM((2, size // 2, 2 * size), bf16),
                pltpu.VMEM((CHUNKS, n, 2 * n, size // 2), f32),
                pltpu.VMEM((CHUNKS, n, 2 * n, size // 2), f32),
                pltpu.VMEM((2, size, size // 2), f32),
                dma((6,)),
                dma(()),
                dma((4, 8)),
                dma((4, 8)),
                dma((CHUNKS, n)),
                dma((CHUNKS, n)),
                dma((CHUNKS, n)),
                dma((CHUNKS, n)),
            ],
            compiler_params=pltpu.CompilerParams(
                collective_id=0, has_side_effects=True, vmem_limit_bytes=52 * 1024 * 1024
            ),
        )(wave_field.reshape(4, n, n, size), trap_field, *(jnp.asarray(a) for a in arrays))
        image = image.reshape(2, n, half, size).transpose(0, 2, 1, 3).reshape(n, n, size)
        return wave_next.reshape(2, 2, n, n, size), image

    return jax.shard_map(
        body,
        mesh=mesh,
        in_specs=(P(None, None, "gy", "gz", None), P("gy", "gz", None)),
        out_specs=(P(None, None, "gy", "gz", None), P("gy", "gz", None)),
        check_vma=False,
    )
```

```python
import math

import jax
import jax.numpy as jnp
import numpy as np
from jax import lax
from jax.experimental import pallas as pl
from jax.experimental.pallas import tpu as pltpu
from jax.sharding import PartitionSpec as P

MESH = pl.DeviceIdType.MESH

hopping = 1.5
time_step = 0.1
rabi_rate = 0.8
inter_self_first = 0.1
inter_cross = 0.06
inter_self_second = 0.08

CHUNKS = 4


def rotation(angle):
    c, s = np.cos(angle), np.sin(angle)
    return np.stack([np.stack([c, s]), np.stack([-s, c])])


def in_two(table):
    table = table.astype(np.float32)
    high = table.astype(jnp.bfloat16)
    low = (table - high.astype(np.float32)).astype(jnp.bfloat16)
    return np.stack([high, low])


def tables(n):
    size, half = n * n, n // 2
    i = np.arange(size)
    full = rotation(2.0 * np.pi * ((i[:, None] * i[None, :]) % size) / size)
    one = full.reshape(2, 2, n, 2, half, size).transpose(3, 2, 0, 4, 1, 5)
    one = one.reshape(2, size, 2 * size)
    j = np.arange(n)
    small = rotation(2.0 * np.pi * ((j[:, None] * j[None, :]) % n) / n)
    two = np.einsum("opay,zw->aozpyw", small, np.eye(n)).reshape(2 * size, 2 * size)
    three = full.reshape(2, 2, size, n, n).transpose(0, 2, 3, 1, 4).reshape(2 * size, 2 * size)
    turn = 2.0 * np.pi * (j[:, None] * j[None, :]) / size
    turn = np.repeat(turn, n, axis=1)
    twiddle = np.stack([np.cos(turn), np.sin(turn)], axis=1)
    two = np.concatenate([two, twiddle.reshape(n, 2 * size)])
    return in_two(one), in_two(two), in_two(three)


def fourier(values):
    count = len(values)
    if count == 1:
        return values
    even, odd = fourier(values[0::2]), fourier(values[1::2])
    first, second = [], []
    for k in range(count // 2):
        (er, ei), (r, i) = even[k], odd[k]
        if k == 0:
            tr, ti = r, i
        elif 4 * k == count:
            tr, ti = i, -r
        else:
            c, s = math.cos(2.0 * math.pi * k / count), math.sin(2.0 * math.pi * k / count)
            if 8 * k == count:
                tr, ti = c * (r + i), c * (i - r)
            elif 8 * k == 3 * count:
                tr, ti = s * (i - r), -s * (r + i)
            else:
                tr, ti = c * r + s * i, c * i - s * r
        first.append((er + tr, ei + ti))
        second.append((er - tr, ei - ti))
    return first + second


def split(value):
    high = value.astype(jnp.bfloat16)
    return high, (value - high.astype(jnp.float32)).astype(jnp.bfloat16)


def product(table, high, low, dims):
    def dot(a, b):
        return lax.dot_general(a, b, (dims, ((), ())), preferred_element_type=jnp.float32)

    return dot(table[0], high) + (dot(table[0], low) + dot(table[1], high))


NT = ((1,), (1,))
NN = ((1,), (0,))


def kernel(
    n, wave_hbm, trap_hbm, one_hbm, two_hbm, three_hbm,
    next_hbm, image_ref,
    state0, state1, state2, state3, out0, out1, out2, out3, in0, in1, in2, in3, trap, wave_next, field, one, two, three, twiddle,
    sent_y, got_y, mixed, sent_z, got_z, power,
    load_sem, store_sem, halo_send, halo_recv, y_send, y_recv, z_send, z_recv,
):
    size, half = n * n, n // 2
    state = (state0, state1, state2, state3)
    face_out, face_in = (out0, out1, out2, out3), (in0, in1, in2, in3)
    gy, gz = lax.axis_index("gy"), lax.axis_index("gz")

    def in_y(d):
        return (lax.rem(gy + d, n), gz)

    def in_z(d):
        return (gy, lax.rem(gz + d, n))

    loads = [
        pltpu.make_async_copy(wave_hbm, state[0].at[:, pl.ds(1, n)], load_sem.at[0]),
        pltpu.make_async_copy(trap_hbm, trap, load_sem.at[1]),
        pltpu.make_async_copy(one_hbm, one, load_sem.at[2]),
        pltpu.make_async_copy(two_hbm, two, load_sem.at[3]),
        pltpu.make_async_copy(three_hbm, three, load_sem.at[4]),
    ]
    loads[0].start()
    barrier = pltpu.get_barrier_semaphore()

    def greet(d, carry):
        pl.semaphore_signal(barrier, inc=1, device_id=in_y(d), device_id_type=MESH)
        pl.semaphore_signal(barrier, inc=1, device_id=in_z(d), device_id_type=MESH)
        return carry

    lax.fori_loop(1, n, greet, 0)
    for load in loads[1:]:
        load.start()

    groups = ((0, 2), (2, n // 2), (n // 2, n))

    def y_faces(s):
        up = pltpu.make_async_remote_copy(
            src_ref=state[s].at[:, pl.ds(n, 1)], dst_ref=state[s].at[:, pl.ds(0, 1)],
            send_sem=halo_send.at[s, 0], recv_sem=halo_recv.at[s, 0],
            device_id=in_y(1), device_id_type=MESH,
        )
        down = pltpu.make_async_remote_copy(
            src_ref=state[s].at[:, pl.ds(1, 1)], dst_ref=state[s].at[:, pl.ds(n + 1, 1)],
            send_sem=halo_send.at[s, 1], recv_sem=halo_recv.at[s, 1],
            device_id=in_y(n - 1), device_id_type=MESH,
        )
        return up, down

    def z_faces(s, g):
        first, end = groups[g]
        part = pl.ds(first, end - first)
        up = pltpu.make_async_remote_copy(
            src_ref=face_out[s].at[1, part], dst_ref=face_in[s].at[0, part],
            send_sem=halo_send.at[s, 2 + 2 * g], recv_sem=halo_recv.at[s, 2 + 2 * g],
            device_id=in_z(1), device_id_type=MESH,
        )
        down = pltpu.make_async_remote_copy(
            src_ref=face_out[s].at[0, part], dst_ref=face_in[s].at[1, part],
            send_sem=halo_send.at[s, 3 + 2 * g], recv_sem=halo_recv.at[s, 3 + 2 * g],
            device_id=in_z(n - 1), device_id_type=MESH,
        )
        return up, down

    def over_planes(g, do, together=2):
        first, end = groups[g]

        def some(q, carry):
            js = [first + together * q + k for k in range(together)]
            do([(j, j * (n - 1) if g == 0 else j - 1) for j in js])
            return carry

        lax.fori_loop(0, (end - first) // together, some, 0)

    def keep_faces(s, j, i, plane):
        face_out[s][0, j, i : i + 1, :] = plane[0:1]
        face_out[s][1, j, i : i + 1, :] = plane[n - 1 : n]

    loads[0].wait()

    def first_faces(planes):
        for j, y in planes:
            for i in range(4):
                keep_faces(0, j, i, state[0][i, y + 1])

    for g in range(3):
        over_planes(g, first_faces)
    pl.semaphore_wait(barrier, 2 * (n - 1))
    for copy in y_faces(0) + z_faces(0, 0) + z_faces(0, 1) + z_faces(0, 2):
        copy.start()
    loads[1].wait()

    row = lax.broadcasted_iota(jnp.int32, (n, size), 0)

    def slope(s, j, y, components=(0, 1)):
        center = [state[s][i, y + 1] for i in range(4)]
        density = [
            center[0] * center[0] + center[1] * center[1],
            center[2] * center[2] + center[3] * center[3],
        ]
        base = trap[y]
        change = {}
        for c in components:
            own, cross = ((inter_self_first, inter_cross), (inter_cross, inter_self_second))[c]
            level = base + own * density[0] + cross * density[1]
            applied = []
            for i in (2 * c, 2 * c + 1):
                mid = center[i]
                before = face_in[s][0, j, i : i + 1, :]
                after = face_in[s][1, j, i : i + 1, :]
                beside = state[s][i, y + 2] + state[s][i, y]
                beside += jnp.where(row == 0, before, pltpu.roll(mid, 1, 0))
                beside += jnp.where(row == n - 1, after, pltpu.roll(mid, n - 1, 0))
                beside += pltpu.roll(mid, 1, 1) + pltpu.roll(mid, size - 1, 1)
                applied.append(
                    level * mid - hopping * beside - 0.5 * rabi_rate * center[(i + 2) % 4]
                )
            change[2 * c], change[2 * c + 1] = applied[1], -applied[0]
        return change

    for s in range(3):
        step = (0.5 * time_step, 0.5 * time_step, time_step)[s]

        def advance(planes, s=s, step=step):
            made = []
            for j, y in planes:
                for i, change in slope(s, j, y).items():
                    made.append((j, y, i, state[0][i, y + 1] + step * change))
            for j, y, i, new in made:
                state[s + 1][i, y + 1] = new
                keep_faces(s + 1, j, i, new)

        for g in range(3):
            for copy in z_faces(s, g) + (y_faces(s) if g == 0 else ()):
                copy.wait_recv()
            over_planes(g, advance)
            for copy in (y_faces(s + 1) if g == 0 else ()) + z_faces(s + 1, g):
                copy.start()

    def y_copy(ch, d):
        return pltpu.make_async_remote_copy(
            src_ref=sent_y.at[ch, lax.rem(gy + d, n)], dst_ref=got_y.at[ch, gy],
            send_sem=y_send.at[ch, d], recv_sem=y_recv.at[ch, d],
            device_id=in_y(d), device_id_type=MESH,
        )

    def z_copy(ch, d):
        return pltpu.make_async_remote_copy(
            src_ref=sent_z.at[ch, lax.rem(gz + d, n)], dst_ref=got_z.at[ch, gz],
            send_sem=z_send.at[ch, d], recv_sem=z_recv.at[ch, d],
            device_id=in_z(d), device_id_type=MESH,
        )

    def start_all(copy, ch):
        def one_start(j, carry):
            away = j // 2 + 1
            copy(ch, lax.rem(n + away * (1 - 2 * (j % 2)), n)).start()
            return carry

        lax.fori_loop(0, n - 1, one_start, 0)

    def arrived(copy, ch):
        def one_wait(d, carry):
            copy(ch, d).wait_recv()
            return carry

        lax.fori_loop(1, n, one_wait, 0)

    for c in range(2):

        def last(planes, c=c):
            made = []
            for j, y in planes:
                for i, change in slope(3, j, y, (c,)).items():
                    kept = (
                        state[1][i, y + 1] + state[3][i, y + 1] - state[0][i, y + 1]
                        + 2.0 * state[2][i, y + 1]
                    )
                    made.append((y, i, kept * (1.0 / 3.0) + (time_step / 6.0) * change))
            for y, i, new in made:
                wave_next[i, y] = new
                high, low = split(new)
                rows = pl.ds(pl.multiple_of(y * n, n), n)
                field[0, c, rows, (i % 2) * size : (i % 2 + 1) * size] = high
                field[1, c, rows, (i % 2) * size : (i % 2 + 1) * size] = low

        for g in range(3):
            if c == 0:
                for copy in z_faces(3, g) + (y_faces(3) if g == 0 else ()):
                    copy.wait_recv()
            over_planes(g, last)
        if c == 0:
            loads[2].wait()

        def along_x(h, carry, c=c):
            ch = 2 * c + h
            out = product((one[0, h], one[1, h]), field[0, c], field[1, c], NT)
            sent_y[ch] = out.reshape(n, n, size)
            start_all(y_copy, ch)
            got_y[ch, gy] = sent_y[ch, gy]
            return carry

        lax.fori_loop(0, 2, along_x, 0)

    store = pltpu.make_async_copy(wave_next, next_hbm, store_sem)
    store.start()

    loads[3].wait()
    twiddle[...] = two[0, 2 * size :].astype(jnp.float32) + two[1, 2 * size :].astype(jnp.float32)

    def along_y(ch, carry):
        arrived(y_copy, ch)
        lanes = size // 2
        for part in range(2):
            at = slice(part * lanes, (part + 1) * lanes)
            beyond = slice(size + part * lanes, size + (part + 1) * lanes)
            values = [(got_y[ch, s, 0:half, at], got_y[ch, s, half:n, at]) for s in range(n)]
            values = fourier(values)
            for b in range(0, n, 2):
                turned = []
                for k in (b, b + 1):
                    (re, im), cos, sin = values[k], twiddle[k : k + 1, at], twiddle[k : k + 1, beyond]
                    turned.append((re * cos + im * sin, im * cos - re * sin))
                for p in range(2):
                    both = jnp.concatenate([turned[0][p], turned[1][p]], axis=0)
                    high, low = split(both)
                    to = slice(p * size + part * lanes, p * size + (part + 1) * lanes)
                    mixed[0, b * half : (b + 2) * half, to] = high
                    mixed[1, b * half : (b + 2) * half, to] = low
        out = product((two[0, : 2 * size], two[1, : 2 * size]), mixed[0], mixed[1], NT)
        sent_z[ch] = out.reshape(n, 2 * n, size // 2)
        start_all(z_copy, ch)
        got_z[ch, gz] = sent_z[ch, gz]
        return carry

    lax.fori_loop(0, CHUNKS, along_y, 0)

    loads[4].wait()

    for c in range(2):

        def along_z(h, carry, c=c):
            ch = 2 * c + h
            arrived(z_copy, ch)
            high, low = split(got_z[ch].reshape(2 * size, size // 2))
            out = product((three[0], three[1]), high, low, NN)
            re, im = out[:size], out[size:]
            new = re * re + im * im
            if c == 0:
                power[h] = new
            else:
                image_ref[h] = ((power[h] + new) * (1.0 / float(size**3))).T
            return carry

        lax.fori_loop(0, 2, along_z, 0)

    for s in range(4):
        for copy in y_faces(s) + z_faces(s, 0) + z_faces(s, 1) + z_faces(s, 2):
            copy.wait_send()

    def sent(j, carry):
        for ch in range(CHUNKS):
            y_copy(ch, j).wait_send()
            z_copy(ch, j).wait_send()
        return carry

    lax.fori_loop(1, n, sent, 0)
    store.wait()


def solution(mesh):
    n = mesh.shape["gy"]
    size, half = n * n, n // 2
    arrays = tables(n)

    def body(wave_field, trap_field):
        f32, bf16 = jnp.float32, jnp.bfloat16
        dma = pltpu.SemaphoreType.DMA
        wave_next, image = pl.pallas_call(
            lambda *refs: kernel(n, *refs),
            out_shape=(
                jax.ShapeDtypeStruct((4, n, n, size), f32),
                jax.ShapeDtypeStruct((2, size // 2, size), f32),
            ),
            in_specs=[pl.BlockSpec(memory_space=pltpu.HBM)] * 5,
            out_specs=(
                pl.BlockSpec(memory_space=pltpu.HBM),
                pl.BlockSpec(memory_space=pltpu.VMEM),
            ),
            scratch_shapes=[
                *[pltpu.VMEM((4, n + 2, n, size), f32)] * 4,
                *[pltpu.VMEM((2, n, 4, size), f32)] * 8,
                pltpu.VMEM((n, n, size), f32),
                pltpu.VMEM((4, n, n, size), f32),
                pltpu.VMEM((2, 2, size, 2 * size), bf16),
                pltpu.VMEM((2, 2, size, 2 * size), bf16),
                pltpu.VMEM((2, 2 * size + n, 2 * size), bf16),
                pltpu.VMEM((2, 2 * size, 2 * size), bf16),
                pltpu.VMEM((n, 2 * size), f32),
                pltpu.VMEM((CHUNKS, n, n, size), f32),
                pltpu.VMEM((CHUNKS, n, n, size), f32),
                pltpu.VMEM((2, size // 2, 2 * size), bf16),
                pltpu.VMEM((CHUNKS, n, 2 * n, size // 2), f32),
                pltpu.VMEM((CHUNKS, n, 2 * n, size // 2), f32),
                pltpu.VMEM((2, size, size // 2), f32),
                dma((5,)),
                dma(()),
                dma((4, 8)),
                dma((4, 8)),
                dma((CHUNKS, n)),
                dma((CHUNKS, n)),
                dma((CHUNKS, n)),
                dma((CHUNKS, n)),
            ],
            compiler_params=pltpu.CompilerParams(
                collective_id=0, has_side_effects=True, vmem_limit_bytes=52 * 1024 * 1024
            ),
        )(wave_field.reshape(4, n, n, size), pltpu.with_memory_space_constraint(trap_field, pltpu.HBM), *(jnp.asarray(a) for a in arrays))
        image = image.reshape(2, n, half, size).transpose(0, 2, 1, 3).reshape(n, n, size)
        return wave_next.reshape(2, 2, n, n, size), image

    return jax.shard_map(
        body,
        mesh=mesh,
        in_specs=(P(None, None, "gy", "gz", None), P("gy", "gz", None)),
        out_specs=(P(None, None, "gy", "gz", None), P("gy", "gz", None)),
        check_vma=False,
    )
```

```python
import math

import jax
import jax.numpy as jnp
import numpy as np
from jax import lax
from jax.experimental import pallas as pl
from jax.experimental.pallas import tpu as pltpu
from jax.sharding import PartitionSpec as P

MESH = pl.DeviceIdType.MESH

hopping = 1.5
time_step = 0.1
rabi_rate = 0.8
inter_self_first = 0.1
inter_cross = 0.06
inter_self_second = 0.08

CHUNKS = 4


def rotation(angle):
    c, s = np.cos(angle), np.sin(angle)
    return np.stack([np.stack([c, s]), np.stack([-s, c])])


def in_two(table):
    table = table.astype(np.float32)
    high = table.astype(jnp.bfloat16)
    low = (table - high.astype(np.float32)).astype(jnp.bfloat16)
    return np.stack([high, low])


def tables(n):
    size, half = n * n, n // 2
    i = np.arange(size)
    full = rotation(2.0 * np.pi * ((i[:, None] * i[None, :]) % size) / size)
    one = full.reshape(2, 2, n, 2, half, size).transpose(3, 2, 0, 4, 1, 5)
    one = one.reshape(2, size, 2 * size)
    j = np.arange(n)
    small = rotation(2.0 * np.pi * ((j[:, None] * j[None, :]) % n) / n)
    two = np.einsum("opay,zw->aozpyw", small, np.eye(n)).reshape(2 * size, 2 * size)
    three = full.reshape(2, 2, size, n, n).transpose(0, 2, 3, 1, 4).reshape(2 * size, 2 * size)
    turn = 2.0 * np.pi * (j[:, None] * j[None, :]) / size
    turn = np.repeat(turn, n, axis=1)
    twiddle = np.stack([np.cos(turn), np.sin(turn)], axis=1)
    two = np.concatenate([two, twiddle.reshape(n, 2 * size)])
    return in_two(one), in_two(two), in_two(three)


def fourier(values):
    count = len(values)
    if count == 1:
        return values
    even, odd = fourier(values[0::2]), fourier(values[1::2])
    first, second = [], []
    for k in range(count // 2):
        (er, ei), (r, i) = even[k], odd[k]
        if k == 0:
            tr, ti = r, i
        elif 4 * k == count:
            tr, ti = i, -r
        else:
            c, s = math.cos(2.0 * math.pi * k / count), math.sin(2.0 * math.pi * k / count)
            if 8 * k == count:
                tr, ti = c * (r + i), c * (i - r)
            elif 8 * k == 3 * count:
                tr, ti = s * (i - r), -s * (r + i)
            else:
                tr, ti = c * r + s * i, c * i - s * r
        first.append((er + tr, ei + ti))
        second.append((er - tr, ei - ti))
    return first + second


def split(value):
    high = value.astype(jnp.bfloat16)
    return high, (value - high.astype(jnp.float32)).astype(jnp.bfloat16)


def product(table, high, low, dims):
    def dot(a, b):
        return lax.dot_general(a, b, (dims, ((), ())), preferred_element_type=jnp.float32)

    return dot(table[0], high) + (dot(table[0], low) + dot(table[1], high))


NT = ((1,), (1,))
NN = ((1,), (0,))


def kernel(
    n, wave_hbm, trap_hbm, one_hbm, two_hbm, three_hbm,
    next_hbm, image_ref,
    state0, state1, state2, state3, out0, out1, out2, out3, in0, in1, in2, in3, trap, wave_next, field, one, two, three, twiddle,
    sent_y, got_y, mixed, sent_z, got_z, power,
    load_sem, store_sem, halo_send, halo_recv, y_send, y_recv, z_send, z_recv,
):
    size, half = n * n, n // 2
    state = (state0, state1, state2, state3)
    face_out, face_in = (out0, out1, out2, out3), (in0, in1, in2, in3)
    gy, gz = lax.axis_index("gy"), lax.axis_index("gz")

    def in_y(d):
        return (lax.rem(gy + d, n), gz)

    def in_z(d):
        return (gy, lax.rem(gz + d, n))

    loads = [
        pltpu.make_async_copy(wave_hbm, state[0].at[:, pl.ds(1, n)], load_sem.at[0]),
        pltpu.make_async_copy(trap_hbm, trap, load_sem.at[1]),
        pltpu.make_async_copy(one_hbm, one, load_sem.at[2]),
        pltpu.make_async_copy(two_hbm, two, load_sem.at[3]),
        pltpu.make_async_copy(three_hbm, three, load_sem.at[4]),
    ]
    loads[0].start()
    barrier = pltpu.get_barrier_semaphore()

    def greet(d, carry):
        pl.semaphore_signal(barrier, inc=1, device_id=in_y(d), device_id_type=MESH)
        pl.semaphore_signal(barrier, inc=1, device_id=in_z(d), device_id_type=MESH)
        return carry

    lax.fori_loop(1, n, greet, 0)
    for load in loads[1:]:
        load.start()

    groups = ((0, 2), (2, n // 2), (n // 2, n))

    def y_faces(s):
        up = pltpu.make_async_remote_copy(
            src_ref=state[s].at[:, pl.ds(n, 1)], dst_ref=state[s].at[:, pl.ds(0, 1)],
            send_sem=halo_send.at[s, 0], recv_sem=halo_recv.at[s, 0],
            device_id=in_y(1), device_id_type=MESH,
        )
        down = pltpu.make_async_remote_copy(
            src_ref=state[s].at[:, pl.ds(1, 1)], dst_ref=state[s].at[:, pl.ds(n + 1, 1)],
            send_sem=halo_send.at[s, 1], recv_sem=halo_recv.at[s, 1],
            device_id=in_y(n - 1), device_id_type=MESH,
        )
        return up, down

    def z_faces(s, g):
        first, end = groups[g]
        part = pl.ds(first, end - first)
        up = pltpu.make_async_remote_copy(
            src_ref=face_out[s].at[1, part], dst_ref=face_in[s].at[0, part],
            send_sem=halo_send.at[s, 2 + 2 * g], recv_sem=halo_recv.at[s, 2 + 2 * g],
            device_id=in_z(1), device_id_type=MESH,
        )
        down = pltpu.make_async_remote_copy(
            src_ref=face_out[s].at[0, part], dst_ref=face_in[s].at[1, part],
            send_sem=halo_send.at[s, 3 + 2 * g], recv_sem=halo_recv.at[s, 3 + 2 * g],
            device_id=in_z(n - 1), device_id_type=MESH,
        )
        return up, down

    def over_planes(g, do, together=2):
        first, end = groups[g]
        if (end - first) % 4 == 0:
            together = 4

        def some(q, carry):
            js = [first + together * q + k for k in range(together)]
            do([(j, j * (n - 1) if g == 0 else j - 1) for j in js])
            return carry

        lax.fori_loop(0, (end - first) // together, some, 0)

    def keep_faces(s, j, i, plane):
        face_out[s][0, j, i : i + 1, :] = plane[0:1]
        face_out[s][1, j, i : i + 1, :] = plane[n - 1 : n]

    loads[0].wait()

    def first_faces(planes):
        for j, y in planes:
            for i in range(4):
                keep_faces(0, j, i, state[0][i, y + 1])

    for g in range(3):
        over_planes(g, first_faces)
    pl.semaphore_wait(barrier, 2 * (n - 1))
    for copy in y_faces(0) + z_faces(0, 0) + z_faces(0, 1) + z_faces(0, 2):
        copy.start()
    loads[1].wait()

    row = lax.broadcasted_iota(jnp.int32, (n, size), 0)

    def slope(s, j, y, components=(0, 1)):
        center = [state[s][i, y + 1] for i in range(4)]
        density = [
            center[0] * center[0] + center[1] * center[1],
            center[2] * center[2] + center[3] * center[3],
        ]
        base = trap[y]
        change = {}
        for c in components:
            own, cross = ((inter_self_first, inter_cross), (inter_cross, inter_self_second))[c]
            level = base + own * density[0] + cross * density[1]
            applied = []
            for i in (2 * c, 2 * c + 1):
                mid = center[i]
                before = face_in[s][0, j, i : i + 1, :]
                after = face_in[s][1, j, i : i + 1, :]
                beside = state[s][i, y + 2] + state[s][i, y]
                beside += jnp.where(row == 0, before, pltpu.roll(mid, 1, 0))
                beside += jnp.where(row == n - 1, after, pltpu.roll(mid, n - 1, 0))
                beside += pltpu.roll(mid, 1, 1) + pltpu.roll(mid, size - 1, 1)
                applied.append(
                    level * mid - hopping * beside - 0.5 * rabi_rate * center[(i + 2) % 4]
                )
            change[2 * c], change[2 * c + 1] = applied[1], -applied[0]
        return change

    for s in range(3):
        step = (0.5 * time_step, 0.5 * time_step, time_step)[s]

        def advance(planes, s=s, step=step):
            made = []
            for j, y in planes:
                for i, change in slope(s, j, y).items():
                    made.append((j, y, i, state[0][i, y + 1] + step * change))
            for j, y, i, new in made:
                state[s + 1][i, y + 1] = new
                keep_faces(s + 1, j, i, new)

        for g in range(3):
            for copy in z_faces(s, g) + (y_faces(s) if g == 0 else ()):
                copy.wait_recv()
            over_planes(g, advance)
            for copy in (y_faces(s + 1) if g == 0 else ()) + z_faces(s + 1, g):
                copy.start()

    def y_copy(ch, d):
        return pltpu.make_async_remote_copy(
            src_ref=sent_y.at[ch, lax.rem(gy + d, n)], dst_ref=got_y.at[ch, gy],
            send_sem=y_send.at[ch, d], recv_sem=y_recv.at[ch, d],
            device_id=in_y(d), device_id_type=MESH,
        )

    def z_copy(ch, d):
        return pltpu.make_async_remote_copy(
            src_ref=sent_z.at[ch, lax.rem(gz + d, n)], dst_ref=got_z.at[ch, gz],
            send_sem=z_send.at[ch, d], recv_sem=z_recv.at[ch, d],
            device_id=in_z(d), device_id_type=MESH,
        )

    def start_all(copy, ch):
        def one_start(j, carry):
            away = j // 2 + 1
            copy(ch, lax.rem(n + away * (1 - 2 * (j % 2)), n)).start()
            return carry

        lax.fori_loop(0, n - 1, one_start, 0)

    def arrived(copy, ch):
        def one_wait(d, carry):
            copy(ch, d).wait_recv()
            return carry

        lax.fori_loop(1, n, one_wait, 0)

    for c in range(2):

        def last(planes, c=c):
            made = []
            for j, y in planes:
                for i, change in slope(3, j, y, (c,)).items():
                    kept = (
                        state[1][i, y + 1] + state[3][i, y + 1] - state[0][i, y + 1]
                        + 2.0 * state[2][i, y + 1]
                    )
                    made.append((y, i, kept * (1.0 / 3.0) + (time_step / 6.0) * change))
            for y, i, new in made:
                wave_next[i, y] = new
                high, low = split(new)
                rows = pl.ds(pl.multiple_of(y * n, n), n)
                field[0, c, rows, (i % 2) * size : (i % 2 + 1) * size] = high
                field[1, c, rows, (i % 2) * size : (i % 2 + 1) * size] = low

        for g in range(3):
            if c == 0:
                for copy in z_faces(3, g) + (y_faces(3) if g == 0 else ()):
                    copy.wait_recv()
            over_planes(g, last)
        if c == 0:
            loads[2].wait()

        def along_x(h, carry, c=c):
            ch = 2 * c + h
            out = product((one[0, h], one[1, h]), field[0, c], field[1, c], NT)
            sent_y[ch] = out.reshape(n, n, size)
            start_all(y_copy, ch)
            got_y[ch, gy] = sent_y[ch, gy]
            return carry

        lax.fori_loop(0, 2, along_x, 0)

    store = pltpu.make_async_copy(wave_next, next_hbm, store_sem)
    store.start()

    loads[3].wait()
    twiddle[...] = two[0, 2 * size :].astype(jnp.float32) + two[1, 2 * size :].astype(jnp.float32)

    def along_y(ch, carry):
        arrived(y_copy, ch)
        lanes = size // 2
        for part in range(2):
            at = slice(part * lanes, (part + 1) * lanes)
            beyond = slice(size + part * lanes, size + (part + 1) * lanes)
            values = [(got_y[ch, s, 0:half, at], got_y[ch, s, half:n, at]) for s in range(n)]
            values = fourier(values)
            for b in range(0, n, 2):
                turned = []
                for k in (b, b + 1):
                    (re, im), cos, sin = values[k], twiddle[k : k + 1, at], twiddle[k : k + 1, beyond]
                    turned.append((re * cos + im * sin, im * cos - re * sin))
                for p in range(2):
                    both = jnp.concatenate([turned[0][p], turned[1][p]], axis=0)
                    high, low = split(both)
                    to = slice(p * size + part * lanes, p * size + (part + 1) * lanes)
                    mixed[0, b * half : (b + 2) * half, to] = high
                    mixed[1, b * half : (b + 2) * half, to] = low
        out = product((two[0, : 2 * size], two[1, : 2 * size]), mixed[0], mixed[1], NT)
        sent_z[ch] = out.reshape(n, 2 * n, size // 2)
        start_all(z_copy, ch)
        got_z[ch, gz] = sent_z[ch, gz]
        return carry

    lax.fori_loop(0, CHUNKS, along_y, 0)

    loads[4].wait()

    for c in range(2):

        def along_z(h, carry, c=c):
            ch = 2 * c + h
            arrived(z_copy, ch)
            high, low = split(got_z[ch].reshape(2 * size, size // 2))
            out = product((three[0], three[1]), high, low, NN)
            re, im = out[:size], out[size:]
            new = re * re + im * im
            if c == 0:
                power[h] = new
            else:
                image_ref[h] = ((power[h] + new) * (1.0 / float(size**3))).T
            return carry

        lax.fori_loop(0, 2, along_z, 0)

    for s in range(4):
        for copy in y_faces(s) + z_faces(s, 0) + z_faces(s, 1) + z_faces(s, 2):
            copy.wait_send()

    def sent(j, carry):
        for ch in range(CHUNKS):
            y_copy(ch, j).wait_send()
            z_copy(ch, j).wait_send()
        return carry

    lax.fori_loop(1, n, sent, 0)
    store.wait()


def solution(mesh):
    n = mesh.shape["gy"]
    size, half = n * n, n // 2
    arrays = tables(n)

    def body(wave_field, trap_field):
        f32, bf16 = jnp.float32, jnp.bfloat16
        dma = pltpu.SemaphoreType.DMA
        wave_next, image = pl.pallas_call(
            lambda *refs: kernel(n, *refs),
            out_shape=(
                jax.ShapeDtypeStruct((4, n, n, size), f32),
                jax.ShapeDtypeStruct((2, size // 2, size), f32),
            ),
            in_specs=[pl.BlockSpec(memory_space=pltpu.HBM)] * 5,
            out_specs=(
                pl.BlockSpec(memory_space=pltpu.HBM),
                pl.BlockSpec(memory_space=pltpu.VMEM),
            ),
            scratch_shapes=[
                *[pltpu.VMEM((4, n + 2, n, size), f32)] * 4,
                *[pltpu.VMEM((2, n, 4, size), f32)] * 8,
                pltpu.VMEM((n, n, size), f32),
                pltpu.VMEM((4, n, n, size), f32),
                pltpu.VMEM((2, 2, size, 2 * size), bf16),
                pltpu.VMEM((2, 2, size, 2 * size), bf16),
                pltpu.VMEM((2, 2 * size + n, 2 * size), bf16),
                pltpu.VMEM((2, 2 * size, 2 * size), bf16),
                pltpu.VMEM((n, 2 * size), f32),
                pltpu.VMEM((CHUNKS, n, n, size), f32),
                pltpu.VMEM((CHUNKS, n, n, size), f32),
                pltpu.VMEM((2, size // 2, 2 * size), bf16),
                pltpu.VMEM((CHUNKS, n, 2 * n, size // 2), f32),
                pltpu.VMEM((CHUNKS, n, 2 * n, size // 2), f32),
                pltpu.VMEM((2, size, size // 2), f32),
                dma((5,)),
                dma(()),
                dma((4, 8)),
                dma((4, 8)),
                dma((CHUNKS, n)),
                dma((CHUNKS, n)),
                dma((CHUNKS, n)),
                dma((CHUNKS, n)),
            ],
            compiler_params=pltpu.CompilerParams(
                collective_id=0, has_side_effects=True, vmem_limit_bytes=52 * 1024 * 1024
            ),
        )(wave_field.reshape(4, n, n, size), pltpu.with_memory_space_constraint(trap_field, pltpu.HBM), *(jnp.asarray(a) for a in arrays))
        image = image.reshape(2, n, half, size).transpose(0, 2, 1, 3).reshape(n, n, size)
        return wave_next.reshape(2, 2, n, n, size), image

    return jax.shard_map(
        body,
        mesh=mesh,
        in_specs=(P(None, None, "gy", "gz", None), P("gy", "gz", None)),
        out_specs=(P(None, None, "gy", "gz", None), P("gy", "gz", None)),
        check_vma=False,
    )
```
